32 devices in a mesh: groups: 2 (over y), seq: 4 (over z), chan: 4 (over x, core).
Axes of the slice: x: 2, y: 2, z: 4, core: 2. Of those that a mesh axis runs over, the one named last changes fastest.
Arguments:
- tokens: bfloat16 [8, 2, 128, 4096], P(('groups', 'seq'), None, None, 'chan'), parts along dimension 0, may hold values from -6 to 6
- w_up: bfloat16 [4096, 4096], P(None, 'chan'), may hold values from -0.09375 to 0.09375
- w_out: bfloat16 [4096, 4096], P('chan'), may hold values from -0.09375 to 0.09375
- rpe_in_w: float32 [64], replicated, may hold values from -1 to 128
- rpe_in_b: float32 [64], replicated, may hold values from -128 to 2
- rpe_mid_w: float32 [64, 64], replicated, may hold values from -32 to 32
- rpe_out_w: float32 [64, 2048], replicated, may hold values from -0.75 to 0.75
- decay_rate: float32 [2048], replicated, may hold values from 0.00029296876 to 0.05
- conv_taps: float32 [5, 2048], replicated, may hold values from -3 to 3
- chan_map: int32 [4096], replicated, may hold values from 0 to 2047
Outputs:
- mixed: bfloat16 [8, 2, 128, 4096], P(('groups', 'seq'), None, None, 'chan'), parts along dimension 0
The draws below stay inside these ranges and needn't reach their ends.
There are 2 independent parts, one for each index of `groups`. The reference program is written for one: setup_inputs(seed, part) draws one part's arguments, and reference() takes and returns one part's arrays. A program takes and returns all parts, laid end to end along the dimension named above; an argument that names none is the same for every part. Nothing has to cross between parts.
All inputs are finite; a program needn't handle non-finite values.
Results may differ from the reference program's by a relative error of at most 0.0085.
Values may be sent and summed in bfloat16 or wider, within the bound.
A program may use at most 192 MiB of HBM per device.

```python
import math
import jax
import jax.numpy as jnp
from jax import lax

C = 4096
C_OLD = 2048
R = 64
KC = 5
BLK = 128
SEQ_LEN = 1024
N_SEQ = 4


def encoder_parts(key):
    base_key = jax.random.fold_in(key, 7)
    key_list = jax.random.split(base_key, 7)
    kink_count = R - 1
    offset_phase = jax.random.uniform(key_list[0], (), jnp.float32)
    scale_factor = jnp.exp(jax.random.uniform(key_list[1], (kink_count,), jnp.float32, math.log(0.5), math.log(2.0)))
    kink_start = (jnp.arange(kink_count, dtype=jnp.int32).astype(jnp.float32) + offset_phase) / kink_count
    slope_input = kink_count * scale_factor
    const_weight = jax.random.uniform(key_list[2], (1,), jnp.float32, -0.2, 0.2)
    const_bias = jax.random.uniform(key_list[3], (1,), jnp.float32, 1.0, 2.0)
    input_weights = jnp.concatenate([const_weight, slope_input])
    input_biases = jnp.concatenate([const_bias, -slope_input * kink_start])
    column_scale = 2.5 * jax.random.truncated_normal(key_list[4], -3.0, 3.0, (R,), jnp.float32)
    level_value = jax.random.uniform(key_list[6], (R,), jnp.float32, 0.05, 0.95)
    edge_index = jnp.arange(kink_count, dtype=jnp.int32)
    sign_rows = jnp.where(edge_index == 0, 1.0, jnp.where(edge_index % 2 == 1, -2.0, 2.0)).astype(jnp.float32)
    middle_rows = (sign_rows / scale_factor)[:, None] * column_scale[None, :]
    top_row = (-level_value * column_scale / const_bias[0])[None, :]
    middle_weights = jnp.concatenate([top_row, middle_rows], axis=0)
    return (input_weights, input_biases, middle_weights)


def draw_rpe_in_w(key, part):
    return encoder_parts(key)[0]


def draw_rpe_in_b(key, part):
    return encoder_parts(key)[1]


def draw_rpe_mid_w(key, part):
    return encoder_parts(key)[2]


def plant(entries, rng, least, top_value):
    place = [jax.random.randint(jax.random.fold_in(rng, axis), (), 0, length) for axis, length in enumerate(entries.shape)]
    widest = entries.shape.index(max(entries.shape))
    neighbour = place[:widest] + [(place[widest] + 1) % entries.shape[widest]] + place[widest + 1:]
    return entries.at[tuple(place)].set(least).at[tuple(neighbour)].set(top_value)


def shard_levels(own_key, extent, cuts, smallest, largest):
    loudness, own = 1.0, jax.random.fold_in(own_key, 6)
    for dim, blocks in cuts:
        heights = jnp.exp(jax.random.uniform(jax.random.fold_in(own, dim), (blocks,), jnp.float32, smallest / len(cuts), largest / len(cuts)))
        loudness = loudness * jnp.repeat(heights, extent[dim] // blocks).reshape([-1 if axis == dim else 1 for axis in range(len(extent))])
    return loudness


def scatter_about(rng, dims, spread, limit, shards=(), kind=jnp.bfloat16):
    values = spread * jax.random.normal(rng, dims, jnp.float32)
    if shards:
        values = values * shard_levels(rng, dims, shards, -0.22, 0.18)
    return jnp.clip(values, -limit, limit).astype(kind)


def setup_inputs(seed: int = 0, part: int = 0) -> dict:
    streams_of = jax.random.split(jax.random.key(seed), 11)
    part_keys = jax.random.split(jax.random.fold_in(streams_of[10], part), 11)
    return {
        "tokens": scatter_about(part_keys[0], (N_SEQ, 2, BLK, C), 1.0, 6.0, ((0, 4), (3, 4))),
        "w_up": scatter_about(streams_of[1], (C, C), C ** -0.5, 0.09375, ((1, 4),)),
        "w_out": scatter_about(streams_of[2], (C, C), C ** -0.5, 0.09375, ((0, 4),)),
        "rpe_in_w": draw_rpe_in_w(jax.random.fold_in(streams_of[10], 71), part),
        "rpe_in_b": draw_rpe_in_b(jax.random.fold_in(streams_of[10], 71), part),
        "rpe_mid_w": draw_rpe_mid_w(jax.random.fold_in(streams_of[10], 71), part),
        "rpe_out_w": scatter_about(streams_of[6], (R, C_OLD), R ** -0.5, 0.75, (), jnp.float32),
        "decay_rate": jnp.clip(jnp.exp(jax.random.uniform(streams_of[7], (C_OLD,), jnp.float32, math.log(0.00029296876), math.log(0.05))), 0.00029296876, 0.05),
        "conv_taps": scatter_about(streams_of[8], (KC, C_OLD), 0.5, 3.0, (), jnp.float32),
        "chan_map": plant(jax.random.randint(streams_of[9], (C,), 0, C_OLD), jax.random.fold_in(streams_of[9], 1), 0, C_OLD - 1).astype(jnp.int32),
    }


def reference(tokens, w_up, w_out, rpe_in_w, rpe_in_b, rpe_mid_w, rpe_out_w, decay_rate, conv_taps, chan_map):
    high = lax.Precision.HIGHEST
    seq_x = jnp.concatenate([tokens[:, 0], tokens[::-1, 1]], axis=0).reshape(SEQ_LEN, C)
    counts = lax.optimization_barrier(jnp.sum((chan_map[:, None] == chan_map[None, :]).astype(jnp.float32), axis=1))
    taps_new = conv_taps[:, chan_map]
    rates = decay_rate[chan_map]
    x_float = seq_x.astype(jnp.float32)
    padded = jnp.concatenate([jnp.zeros((KC - 1, C), jnp.float32), x_float], axis=0)
    conv = jnp.zeros((SEQ_LEN, C), jnp.float32)
    for shift_m in range(KC):
        conv = conv + taps_new[shift_m][None, :] * padded[KC - 1 - shift_m:KC - 1 - shift_m + SEQ_LEN]
    v_data = conv.astype(jnp.bfloat16)
    positions = jnp.arange(SEQ_LEN, dtype=jnp.int32).astype(jnp.float32)
    first = jax.nn.relu((positions / SEQ_LEN)[:, None] * rpe_in_w[None, :] + rpe_in_b[None, :])
    second = jax.nn.relu(jnp.dot(first, rpe_mid_w, precision=high))
    encoded = jnp.dot(second, rpe_out_w[:, chan_map], precision=high)
    gain = jnp.sqrt(2.0 * rates / (1.0 - jnp.exp(-2.0 * rates * SEQ_LEN)))
    kernel = encoded * jnp.exp(-rates[None, :] * positions[:, None]) * gain[None, :]
    v_spec = jnp.fft.rfft(v_data.astype(jnp.float32), n=2 * SEQ_LEN, axis=0)
    k_spec = jnp.fft.rfft(kernel, n=2 * SEQ_LEN, axis=0)
    toep = jnp.fft.irfft(v_spec * k_spec, n=2 * SEQ_LEN, axis=0)[:SEQ_LEN]
    up_pre = jnp.dot(seq_x, w_up, preferred_element_type=jnp.float32)
    hidden = (jax.nn.silu(up_pre) * toep / counts[None, :]).astype(jnp.bfloat16)
    result = jnp.dot(hidden, w_out, preferred_element_type=jnp.float32).astype(jnp.bfloat16)
    blocks = result.reshape(2 * N_SEQ, BLK, C)
    return jnp.stack([blocks[:N_SEQ], blocks[N_SEQ:][::-1]], axis=1)
```

```python
import math

import jax
import jax.numpy as jnp
import numpy as np
from jax import lax
from jax.experimental import pallas as pl
from jax.experimental.pallas import tpu as pltpu
from jax.sharding import PartitionSpec as P

HIGH = lax.Precision.HIGHEST


def shifted(x, axis, by):
    length = lax.axis_size(axis)
    pairs = [(i, i + by) for i in range(length) if 0 <= i + by < length]
    return lax.ppermute(x, axis, pairs)


def dft_tables(block_len):
    period_len = 2 * block_len
    freq_index = jnp.arange(block_len + 1, dtype=jnp.int32)[:, None]
    time_index = jnp.arange(block_len, dtype=jnp.int32)[None, :]
    angles = (freq_index * time_index % period_len).astype(jnp.float32) * (
        2.0 * math.pi / period_len
    )
    forward = jnp.concatenate([jnp.cos(angles), -jnp.sin(angles)], axis=0)
    weights = (
        jnp.where((freq_index == 0) | (freq_index == block_len), 1.0, 2.0).astype(jnp.float32)
        / period_len
    )
    inverse = jnp.concatenate(
        [(weights * jnp.cos(angles)).T, (-weights * jnp.sin(angles)).T], axis=1
    )
    sign_flip = jnp.where(freq_index[:, 0] % 2 == 0, 1.0, -1.0).astype(jnp.float32)
    return (forward, inverse, sign_flip)


def spectra_of(forward, blocks):
    freq_count = forward.shape[0] // 2
    spec = jnp.einsum("gb,hbc->hgc", forward, blocks, precision=HIGH)
    return spec.reshape(blocks.shape[0], 2, freq_count, blocks.shape[2])


def data_spectra(fwd_upper, fwd_lower, blocks):
    freq_count = fwd_upper.shape[0] // 2
    spec = jnp.einsum("gb,hbc->hgc", fwd_upper, blocks, preferred_element_type=jnp.float32)
    spec = spec + jnp.einsum("gb,hbc->hgc", fwd_lower, blocks, preferred_element_type=jnp.float32)
    return spec.reshape(blocks.shape[0], 2, freq_count, blocks.shape[2])


def accumulate(acc, spec_pair, source, own_ids, kernel_spec, total_blocks):
    src_ids = jnp.stack([source, total_blocks - 1 - source])
    lags = own_ids[:, None] - src_ids[None, :]
    valid = (lags >= 0).astype(jnp.float32)[:, :, None, None]
    picked = jnp.take(kernel_spec, jnp.clip(lags, 0, total_blocks - 1).reshape(-1), axis=0)
    picked = picked.reshape((2, 2) + kernel_spec.shape[1:])
    kern_real = picked[:, :, 0]
    kern_imag = picked[:, :, 1]
    data_real = spec_pair[None, :, 0]
    data_imag = spec_pair[None, :, 1]
    real_part = jnp.sum(valid * (kern_real * data_real - kern_imag * data_imag), axis=1)
    imag_part = jnp.sum(valid * (kern_real * data_imag + kern_imag * data_real), axis=1)
    return acc + jnp.stack([real_part, imag_part], axis=1)


def general_shards(
    tokens, w_up, w_out, rpe_in_w, rpe_in_b, rpe_mid_w, rpe_out_w, decay_rate, conv_taps, chan_map
):
    block_len = tokens.shape[2]
    chans = tokens.shape[3]
    seq_count = lax.axis_size("seq")
    seq_pos = lax.axis_index("seq")
    total_blocks = 2 * seq_count
    seq_len = total_blocks * block_len
    rim = conv_taps.shape[0] - 1
    old_count = decay_rate.shape[0]
    hidden_dim = rpe_out_w.shape[0]
    map_local = lax.dynamic_slice_in_dim(chan_map, lax.axis_index("chan") * chans, chans)
    counts = jnp.sum((map_local[:, None] == chan_map[None, :]).astype(jnp.float32), axis=1)
    one_hot = (jnp.arange(old_count, dtype=jnp.int32)[:, None] == map_local[None, :]).astype(
        jnp.float32
    )
    table = jnp.concatenate([rpe_out_w, decay_rate[None, :], conv_taps], axis=0)
    selected = jnp.dot(table, one_hot, precision=HIGH)
    out_cols = selected[:hidden_dim]
    rates = selected[hidden_dim]
    taps_local = selected[hidden_dim + 1 :]
    x_own = tokens[0]
    prev_low = shifted(tokens[:, 0, block_len - rim :], "seq", 1)[0]
    prev_high = shifted(tokens[:, 1, block_len - rim :], "seq", -1)[0]
    prev_high = jnp.where(seq_pos == seq_count - 1, x_own[0, block_len - rim :], prev_high)
    extended = jnp.stack(
        [
            jnp.concatenate([prev_low, x_own[0]], axis=0),
            jnp.concatenate([prev_high, x_own[1]], axis=0),
        ]
    ).astype(jnp.float32)
    conv = jnp.zeros((2, block_len, chans), jnp.float32)
    for shift_m in range(rim + 1):
        conv = (
            conv
            + taps_local[shift_m][None, None, :]
            * extended[:, rim - shift_m : rim - shift_m + block_len]
        )
    v_data = conv.astype(jnp.bfloat16)
    positions = jnp.arange(seq_len, dtype=jnp.int32).astype(jnp.float32)
    first = jax.nn.relu((positions / seq_len)[:, None] * rpe_in_w[None, :] + rpe_in_b[None, :])
    second = jax.nn.relu(jnp.dot(first, rpe_mid_w, precision=HIGH))
    encoded = jnp.dot(second, out_cols, precision=HIGH)
    gain = jnp.sqrt(2.0 * rates / (1.0 - jnp.exp(-2.0 * rates * seq_len)))
    kernel = encoded * jnp.exp(-rates[None, :] * positions[:, None]) * gain[None, :]
    forward, inverse, sign_flip = dft_tables(block_len)
    fwd_upper = forward.astype(jnp.bfloat16)
    fwd_lower = (forward - fwd_upper.astype(jnp.float32)).astype(jnp.bfloat16)
    half_spec = spectra_of(forward, kernel.reshape(total_blocks, block_len, chans))
    earlier = jnp.concatenate([jnp.zeros_like(half_spec[:1]), half_spec[:-1]], axis=0)
    kernel_spec = half_spec + sign_flip[None, None, :, None] * earlier
    own_ids = jnp.stack([seq_pos, total_blocks - 1 - seq_pos])
    start_acc = jnp.zeros((2, 2, block_len + 1, chans), jnp.float32)
    piece = lax.all_gather(v_data[None], "seq", axis=0, tiled=True)

    def one_source(carry, item):
        offset, blocks = item
        spec_pair = data_spectra(fwd_upper, fwd_lower, blocks)
        return (accumulate(carry, spec_pair, offset, own_ids, kernel_spec, total_blocks), None)

    offsets = jnp.arange(piece.shape[0], dtype=jnp.int32)
    result, _ = lax.scan(one_source, start_acc, (offsets, piece))
    toep = jnp.einsum(
        "tg,agc->atc", inverse, result.reshape(2, 2 * (block_len + 1), chans), precision=HIGH
    )
    up_pre = jnp.einsum(
        "qhbc,cd->qhbd",
        lax.all_gather(tokens, "chan", axis=3, tiled=True),
        w_up,
        preferred_element_type=jnp.float32,
    )
    hidden = (jax.nn.silu(up_pre) * toep[None] / counts[None, None, None, :]).astype(jnp.bfloat16)
    partial_sum = jnp.einsum("qhbc,cd->qhbd", hidden, w_out, preferred_element_type=jnp.float32)
    return lax.psum_scatter(partial_sum, "chan", scatter_dimension=3, tiled=True).astype(
        jnp.bfloat16
    )


BF = jnp.bfloat16
F32 = jnp.float32
LOW = 64


def halves(x):
    upper = x.astype(BF)
    return upper, (x - upper.astype(F32)).astype(BF)


def odd_tables(block_len):
    omega = 2.0 * np.pi * (np.arange(block_len)[:, None] + 0.5) / (2 * block_len)
    lags = np.arange(-block_len, block_len)[None, :]
    kern_table = np.concatenate([np.cos(omega * lags), -np.sin(omega * lags)], axis=0)
    data_table = kern_table[:, block_len:]
    times = np.arange(block_len)[None, :]
    back_table = np.concatenate([np.cos(omega * times), -np.sin(omega * times)], axis=0).T / block_len

    def split(table):
        table = table.astype(np.float32)
        upper = table.astype(BF)
        return upper, (table - upper.astype(np.float32)).astype(BF)

    kern_upper, kern_lower = split(kern_table)
    data_upper, data_lower = split(data_table)
    back_upper, back_lower = split(back_table)
    return (
        np.concatenate([kern_upper, kern_upper, kern_lower], axis=1),
        np.concatenate([data_upper, data_lower], axis=1),
        np.concatenate([back_upper, back_upper, back_lower], axis=1),
    )


def mm(a, b):
    return jnp.dot(a, b, preferred_element_type=F32)


def select_params(table, old_of_own, chan_map_row, hidden_dim):
    rows, old_count = table.shape
    width = old_of_own.shape[1]
    upper = table.astype(BF)
    rest = table - upper.astype(F32)
    middle = rest.astype(BF)
    lower = (rest - middle.astype(F32)).astype(BF)
    one_hot = jnp.where(
        lax.broadcasted_iota(jnp.int32, (old_count, width), 0) == old_of_own, 1.0, 0.0
    ).astype(BF)
    selected = mm(upper, one_hot) + mm(middle, one_hot) + mm(lower, one_hot)
    high_count = -(-old_count // LOW)

    def digits(ids):
        width = ids.shape[1]
        high_hot = jnp.where(
            lax.broadcasted_iota(jnp.int32, (high_count, width), 0) == (ids >> 6), 1.0, 0.0
        )
        low_hot = jnp.where(
            lax.broadcasted_iota(jnp.int32, (LOW, width), 0) == (ids & (LOW - 1)), 1.0, 0.0
        )
        return high_hot, low_hot.astype(BF)

    all_high, all_low = digits(chan_map_row)
    histogram = lax.dot_general(
        all_high.astype(BF), all_low, (((1,), (1,)), ((), ())), preferred_element_type=F32
    )
    own_high, own_low = digits(old_of_own)
    hist_upper, hist_lower = halves(histogram)
    counts = jnp.sum(own_high * (mm(hist_upper, own_low) + mm(hist_lower, own_low)), axis=0, keepdims=True)
    return selected, counts


def toep_kernel_spectra(selected, in_w, in_b, mid_w, kern_table, kspec_ref, seq_len, block_len):
    hidden_dim = mid_w.shape[0]
    width = selected.shape[1]
    rates = selected[hidden_dim : hidden_dim + 1]
    positions = lax.broadcasted_iota(jnp.int32, (seq_len, 1), 0).astype(F32)
    first = jnp.maximum((positions / seq_len) * in_w + in_b, 0.0)
    second = jnp.maximum(jnp.dot(first, mid_w, precision=HIGH, preferred_element_type=F32), 0.0)
    encoded = jnp.dot(second, selected[:hidden_dim], precision=HIGH, preferred_element_type=F32)
    gain = jnp.sqrt(2.0 * rates / (1.0 - jnp.exp(-2.0 * rates * seq_len)))
    kern = encoded * jnp.exp(-rates * positions) * gain
    upper, lower = halves(kern)
    blank = jnp.zeros((block_len, width), BF)
    upper = jnp.concatenate([blank, upper], axis=0)
    lower = jnp.concatenate([blank, lower], axis=0)
    for lag in range(seq_len // block_len):
        span = slice(lag * block_len, (lag + 2) * block_len)
        stacked = jnp.concatenate([upper[span], lower[span], upper[span]], axis=0)
        kspec_ref[lag] = mm(kern_table, stacked)


def toep_body(
    x_ref, table_ref, own_ref, map_ref, in_w_ref, in_b_ref, mid_ref, kt_ref, dt_ref, bt_ref,
    out_ref, kspec_ref, vspec_ref, acc_ref,
):
    total, block_len, width = x_ref.shape
    rim = 4
    hidden_dim = mid_ref.shape[0]
    selected, counts = select_params(table_ref[...], own_ref[...], map_ref[...], hidden_dim)
    toep_kernel_spectra(
        selected, in_w_ref[...], in_b_ref[...], mid_ref[...], kt_ref[...], kspec_ref,
        total * block_len, block_len,
    )
    taps = selected[hidden_dim + 1 : hidden_dim + 2 + rim]
    convolve_blocks(x_ref, taps, dt_ref[...], vspec_ref)
    mix_blocks(kspec_ref, vspec_ref, acc_ref, bt_ref[...], 1.0 / counts, out_ref)


def convolve_blocks(x_ref, taps, data_table, vspec_ref):
    total, block_len, width = x_ref.shape
    rim = taps.shape[0] - 1
    tail = jnp.zeros((8, width), F32)
    for block in range(total):
        own = x_ref[block].astype(F32)
        extended = jnp.concatenate([tail, own], axis=0)
        conv = taps[0:1] * own
        for shift in range(1, rim + 1):
            conv = conv + taps[shift : shift + 1] * extended[8 - shift : 8 - shift + block_len]
        tail = own[block_len - 8 :]
        v_data = conv.astype(BF)
        vspec_ref[block] = mm(data_table, jnp.concatenate([v_data, v_data], axis=0))


def mix_blocks(kspec_ref, vspec_ref, acc_ref, back_table, scale, out_ref):
    total, double_len, width = vspec_ref.shape
    block_len = double_len // 2
    rows = 32

    for block in range(total):

        def chunk(step, carry):
            start = pl.multiple_of(step * rows, rows)
            real_rows = pl.ds(start, rows)
            imag_rows = pl.ds(pl.multiple_of(start + block_len, rows), rows)
            real = jnp.zeros((rows, width), F32)
            imag = jnp.zeros((rows, width), F32)
            for source in range(block + 1):
                k_re = kspec_ref[block - source, real_rows, :]
                k_im = kspec_ref[block - source, imag_rows, :]
                v_re = vspec_ref[source, real_rows, :]
                v_im = vspec_ref[source, imag_rows, :]
                real = real + (k_re * v_re - k_im * v_im)
                imag = imag + (k_re * v_im + k_im * v_re)
            acc_ref[real_rows, :] = real
            acc_ref[imag_rows, :] = imag
            return carry

        lax.fori_loop(0, block_len // rows, chunk, 0)
        upper, lower = halves(acc_ref[...])
        toep = mm(back_table, jnp.concatenate([upper, lower, upper], axis=0))
        out_ref[block] = (toep * scale).astype(out_ref.dtype)


def shards(
    tokens, w_up, w_out, rpe_in_w, rpe_in_b, rpe_mid_w, rpe_out_w, decay_rate, conv_taps, chan_map
):
    _, _, block_len, chans = tokens.shape
    seq_count = lax.axis_size("seq")
    total = 2 * seq_count
    width = chans // seq_count
    start = lax.axis_index("chan") * chans + lax.axis_index("seq") * width
    own = lax.dynamic_slice_in_dim(chan_map, start, width)[None, :]
    table = jnp.concatenate([rpe_out_w, decay_rate[None, :], conv_taps], axis=0)
    table = jnp.concatenate([table, jnp.zeros((-table.shape[0] % 16, table.shape[1]), F32)], axis=0)
    pieces = lax.all_to_all(tokens[0], "seq", split_axis=2, concat_axis=0, tiled=True)
    pieces = pieces.reshape(seq_count, 2, block_len, width)
    ordered = jnp.concatenate([pieces[:, 0], pieces[::-1, 1]], axis=0)
    kern_table, data_table, back_table = odd_tables(block_len)
    toep = pl.pallas_call(
        toep_body,
        out_shape=jax.ShapeDtypeStruct((total, block_len, width), BF),
        in_specs=[pl.BlockSpec(memory_space=pltpu.VMEM)] * 10,
        out_specs=pl.BlockSpec(memory_space=pltpu.VMEM),
        scratch_shapes=[
            pltpu.VMEM((total, 2 * block_len, width), F32),
            pltpu.VMEM((total, 2 * block_len, width), F32),
            pltpu.VMEM((2 * block_len, width), F32),
        ],
        compiler_params=pltpu.CompilerParams(vmem_limit_bytes=48 * 1024 * 1024),
    )(
        ordered, table, own, chan_map[None, :], rpe_in_w[None, :], rpe_in_b[None, :], rpe_mid_w,
        kern_table, data_table, back_table,
    )
    returned = jnp.stack([toep[:seq_count], toep[seq_count:][::-1]], axis=1)
    returned = lax.all_to_all(returned, "seq", split_axis=0, concat_axis=3, tiled=True)[0]
    gathered = lax.all_gather(tokens[0], "chan", axis=2, tiled=True)
    up_pre = jnp.einsum("hbc,cd->hbd", gathered, w_up, preferred_element_type=F32)
    hidden = (jax.nn.silu(up_pre) * returned.astype(F32)).astype(BF)
    partial_sum = jnp.einsum("hbc,cd->hbd", hidden, w_out, preferred_element_type=F32).astype(BF)
    return lax.psum_scatter(partial_sum, "chan", scatter_dimension=2, tiled=True)[None]


def solution(mesh):
    in_specs = (
        P(("groups", "seq"), None, None, "chan"),
        P(None, "chan"),
        P("chan", None),
        P(),
        P(),
        P(),
        P(),
        P(),
        P(),
        P(),
    )
    out_specs = P(("groups", "seq"), None, None, "chan")
    def pick(*arrays):
        width = arrays[0].shape[3] // mesh.shape["seq"]
        return (general_shards if width % 128 else shards)(*arrays)

    return jax.shard_map(pick, mesh=mesh, in_specs=in_specs, out_specs=out_specs, check_vma=False)
```

```python
import functools
import math

import jax
import jax.numpy as jnp
import numpy as np
from jax import lax
from jax.experimental import pallas as pl
from jax.experimental.pallas import tpu as pltpu
from jax.sharding import PartitionSpec as P

HIGH = lax.Precision.HIGHEST


def shifted(x, axis, by):
    length = lax.axis_size(axis)
    pairs = [(i, i + by) for i in range(length) if 0 <= i + by < length]
    return lax.ppermute(x, axis, pairs)


def dft_tables(block_len):
    period_len = 2 * block_len
    freq_index = jnp.arange(block_len + 1, dtype=jnp.int32)[:, None]
    time_index = jnp.arange(block_len, dtype=jnp.int32)[None, :]
    angles = (freq_index * time_index % period_len).astype(jnp.float32) * (
        2.0 * math.pi / period_len
    )
    forward = jnp.concatenate([jnp.cos(angles), -jnp.sin(angles)], axis=0)
    weights = (
        jnp.where((freq_index == 0) | (freq_index == block_len), 1.0, 2.0).astype(jnp.float32)
        / period_len
    )
    inverse = jnp.concatenate(
        [(weights * jnp.cos(angles)).T, (-weights * jnp.sin(angles)).T], axis=1
    )
    sign_flip = jnp.where(freq_index[:, 0] % 2 == 0, 1.0, -1.0).astype(jnp.float32)
    return (forward, inverse, sign_flip)


def spectra_of(forward, blocks):
    freq_count = forward.shape[0] // 2
    spec = jnp.einsum("gb,hbc->hgc", forward, blocks, precision=HIGH)
    return spec.reshape(blocks.shape[0], 2, freq_count, blocks.shape[2])


def data_spectra(fwd_upper, fwd_lower, blocks):
    freq_count = fwd_upper.shape[0] // 2
    spec = jnp.einsum("gb,hbc->hgc", fwd_upper, blocks, preferred_element_type=jnp.float32)
    spec = spec + jnp.einsum("gb,hbc->hgc", fwd_lower, blocks, preferred_element_type=jnp.float32)
    return spec.reshape(blocks.shape[0], 2, freq_count, blocks.shape[2])


def accumulate(acc, spec_pair, source, own_ids, kernel_spec, total_blocks):
    src_ids = jnp.stack([source, total_blocks - 1 - source])
    lags = own_ids[:, None] - src_ids[None, :]
    valid = (lags >= 0).astype(jnp.float32)[:, :, None, None]
    picked = jnp.take(kernel_spec, jnp.clip(lags, 0, total_blocks - 1).reshape(-1), axis=0)
    picked = picked.reshape((2, 2) + kernel_spec.shape[1:])
    kern_real = picked[:, :, 0]
    kern_imag = picked[:, :, 1]
    data_real = spec_pair[None, :, 0]
    data_imag = spec_pair[None, :, 1]
    real_part = jnp.sum(valid * (kern_real * data_real - kern_imag * data_imag), axis=1)
    imag_part = jnp.sum(valid * (kern_real * data_imag + kern_imag * data_real), axis=1)
    return acc + jnp.stack([real_part, imag_part], axis=1)


def general_shards(
    tokens, w_up, w_out, rpe_in_w, rpe_in_b, rpe_mid_w, rpe_out_w, decay_rate, conv_taps, chan_map
):
    block_len = tokens.shape[2]
    chans = tokens.shape[3]
    seq_count = lax.axis_size("seq")
    seq_pos = lax.axis_index("seq")
    total_blocks = 2 * seq_count
    seq_len = total_blocks * block_len
    rim = conv_taps.shape[0] - 1
    old_count = decay_rate.shape[0]
    hidden_dim = rpe_out_w.shape[0]
    map_local = lax.dynamic_slice_in_dim(chan_map, lax.axis_index("chan") * chans, chans)
    counts = jnp.sum((map_local[:, None] == chan_map[None, :]).astype(jnp.float32), axis=1)
    one_hot = (jnp.arange(old_count, dtype=jnp.int32)[:, None] == map_local[None, :]).astype(
        jnp.float32
    )
    table = jnp.concatenate([rpe_out_w, decay_rate[None, :], conv_taps], axis=0)
    selected = jnp.dot(table, one_hot, precision=HIGH)
    out_cols = selected[:hidden_dim]
    rates = selected[hidden_dim]
    taps_local = selected[hidden_dim + 1 :]
    x_own = tokens[0]
    prev_low = shifted(tokens[:, 0, block_len - rim :], "seq", 1)[0]
    prev_high = shifted(tokens[:, 1, block_len - rim :], "seq", -1)[0]
    prev_high = jnp.where(seq_pos == seq_count - 1, x_own[0, block_len - rim :], prev_high)
    extended = jnp.stack(
        [
            jnp.concatenate([prev_low, x_own[0]], axis=0),
            jnp.concatenate([prev_high, x_own[1]], axis=0),
        ]
    ).astype(jnp.float32)
    conv = jnp.zeros((2, block_len, chans), jnp.float32)
    for shift_m in range(rim + 1):
        conv = (
            conv
            + taps_local[shift_m][None, None, :]
            * extended[:, rim - shift_m : rim - shift_m + block_len]
        )
    v_data = conv.astype(jnp.bfloat16)
    positions = jnp.arange(seq_len, dtype=jnp.int32).astype(jnp.float32)
    first = jax.nn.relu((positions / seq_len)[:, None] * rpe_in_w[None, :] + rpe_in_b[None, :])
    second = jax.nn.relu(jnp.dot(first, rpe_mid_w, precision=HIGH))
    encoded = jnp.dot(second, out_cols, precision=HIGH)
    gain = jnp.sqrt(2.0 * rates / (1.0 - jnp.exp(-2.0 * rates * seq_len)))
    kernel = encoded * jnp.exp(-rates[None, :] * positions[:, None]) * gain[None, :]
    forward, inverse, sign_flip = dft_tables(block_len)
    fwd_upper = forward.astype(jnp.bfloat16)
    fwd_lower = (forward - fwd_upper.astype(jnp.float32)).astype(jnp.bfloat16)
    half_spec = spectra_of(forward, kernel.reshape(total_blocks, block_len, chans))
    earlier = jnp.concatenate([jnp.zeros_like(half_spec[:1]), half_spec[:-1]], axis=0)
    kernel_spec = half_spec + sign_flip[None, None, :, None] * earlier
    own_ids = jnp.stack([seq_pos, total_blocks - 1 - seq_pos])
    start_acc = jnp.zeros((2, 2, block_len + 1, chans), jnp.float32)
    piece = lax.all_gather(v_data[None], "seq", axis=0, tiled=True)

    def one_source(carry, item):
        offset, blocks = item
        spec_pair = data_spectra(fwd_upper, fwd_lower, blocks)
        return (accumulate(carry, spec_pair, offset, own_ids, kernel_spec, total_blocks), None)

    offsets = jnp.arange(piece.shape[0], dtype=jnp.int32)
    result, _ = lax.scan(one_source, start_acc, (offsets, piece))
    toep = jnp.einsum(
        "tg,agc->atc", inverse, result.reshape(2, 2 * (block_len + 1), chans), precision=HIGH
    )
    up_pre = jnp.einsum(
        "qhbc,cd->qhbd",
        lax.all_gather(tokens, "chan", axis=3, tiled=True),
        w_up,
        preferred_element_type=jnp.float32,
    )
    hidden = (jax.nn.silu(up_pre) * toep[None] / counts[None, None, None, :]).astype(jnp.bfloat16)
    partial_sum = jnp.einsum("qhbc,cd->qhbd", hidden, w_out, preferred_element_type=jnp.float32)
    return lax.psum_scatter(partial_sum, "chan", scatter_dimension=3, tiled=True).astype(
        jnp.bfloat16
    )


BF = jnp.bfloat16
F32 = jnp.float32
LOW = 64


def halves(x):
    upper = x.astype(BF)
    return upper, (x - upper.astype(F32)).astype(BF)


def odd_tables(block_len):
    omega = 2.0 * np.pi * (np.arange(block_len)[:, None] + 0.5) / (2 * block_len)
    lags = np.arange(-block_len, block_len)[None, :]
    kern_table = np.concatenate([np.cos(omega * lags), -np.sin(omega * lags)], axis=0)
    data_table = kern_table[:, block_len:]
    times = np.arange(block_len)[None, :]
    back_table = np.concatenate([np.cos(omega * times), -np.sin(omega * times)], axis=0).T / block_len

    def split(table):
        table = table.astype(np.float32)
        upper = table.astype(BF)
        return upper, (table - upper.astype(np.float32)).astype(BF)

    kern_upper, kern_lower = split(kern_table)
    data_upper, data_lower = split(data_table)
    back_upper, back_lower = split(back_table)
    return (
        np.concatenate([kern_upper, kern_upper, kern_lower], axis=1),
        np.concatenate([data_upper, data_lower], axis=1),
        np.concatenate([back_upper, back_upper, back_lower], axis=1),
    )


def mm(a, b):
    return jnp.dot(a, b, preferred_element_type=F32)


def select_params(table, old_of_own, chan_map_row, hidden_dim):
    rows, old_count = table.shape
    width = old_of_own.shape[1]
    upper = table.astype(BF)
    rest = table - upper.astype(F32)
    middle = rest.astype(BF)
    lower = (rest - middle.astype(F32)).astype(BF)
    one_hot = jnp.where(
        lax.broadcasted_iota(jnp.int32, (old_count, width), 0) == old_of_own, 1.0, 0.0
    ).astype(BF)
    selected = mm(upper, one_hot) + mm(middle, one_hot) + mm(lower, one_hot)
    high_count = -(-old_count // LOW)

    def digits(ids):
        width = ids.shape[1]
        high_hot = jnp.where(
            lax.broadcasted_iota(jnp.int32, (high_count, width), 0) == (ids >> 6), 1.0, 0.0
        )
        low_hot = jnp.where(
            lax.broadcasted_iota(jnp.int32, (LOW, width), 0) == (ids & (LOW - 1)), 1.0, 0.0
        )
        return high_hot, low_hot.astype(BF)

    all_high, all_low = digits(chan_map_row)
    histogram = lax.dot_general(
        all_high.astype(BF), all_low, (((1,), (1,)), ((), ())), preferred_element_type=F32
    )
    own_high, own_low = digits(old_of_own)
    hist_upper, hist_lower = halves(histogram)
    counts = jnp.sum(own_high * (mm(hist_upper, own_low) + mm(hist_lower, own_low)), axis=0, keepdims=True)
    return selected, counts


def toep_kernel_spectra(selected, in_w, in_b, mid_w, kern_table, kspec_ref, seq_len, block_len):
    hidden_dim = mid_w.shape[0]
    width = selected.shape[1]
    rates = selected[hidden_dim : hidden_dim + 1]
    positions = lax.broadcasted_iota(jnp.int32, (seq_len, 1), 0).astype(F32)
    first = jnp.maximum((positions / seq_len) * in_w + in_b, 0.0)
    second = jnp.maximum(jnp.dot(first, mid_w, precision=HIGH, preferred_element_type=F32), 0.0)
    encoded = jnp.dot(second, selected[:hidden_dim], precision=HIGH, preferred_element_type=F32)
    gain = jnp.sqrt(2.0 * rates / (1.0 - jnp.exp(-2.0 * rates * seq_len)))
    kern = encoded * jnp.exp(-rates * positions) * gain
    upper, lower = halves(kern)
    blank = jnp.zeros((block_len, width), BF)
    upper = jnp.concatenate([blank, upper], axis=0)
    lower = jnp.concatenate([blank, lower], axis=0)
    for lag in range(seq_len // block_len):
        span = slice(lag * block_len, (lag + 2) * block_len)
        stacked = jnp.concatenate([upper[span], lower[span], upper[span]], axis=0)
        kspec_ref[lag] = mm(kern_table, stacked)


def convolve_blocks(x_ref, taps, data_table, vspec_ref):
    seq_count, _, block_len, width = x_ref.shape
    total = 2 * seq_count
    rim = taps.shape[0] - 1
    tail = jnp.zeros((8, width), F32)
    for block in range(total):
        own = x_ref[place_of(block, seq_count)].astype(F32)
        extended = jnp.concatenate([tail, own], axis=0)
        conv = taps[0:1] * own
        for shift in range(1, rim + 1):
            conv = conv + taps[shift : shift + 1] * extended[8 - shift : 8 - shift + block_len]
        tail = own[block_len - 8 :]
        v_data = conv.astype(BF)
        vspec_ref[block] = mm(data_table, jnp.concatenate([v_data, v_data], axis=0))


def place_of(block, seq_count):
    return (block, 0) if block < seq_count else (2 * seq_count - 1 - block, 1)


def mix_block(block, kspec_ref, vspec_ref, acc_ref, back_table):
    total, double_len, width = vspec_ref.shape
    block_len = double_len // 2
    rows = 32

    def chunk(step, carry):
        start = pl.multiple_of(step * rows, rows)
        real_rows = pl.ds(start, rows)
        imag_rows = pl.ds(pl.multiple_of(start + block_len, rows), rows)
        real = jnp.zeros((rows, width), F32)
        imag = jnp.zeros((rows, width), F32)
        for source in range(block + 1):
            k_re = kspec_ref[block - source, real_rows, :]
            k_im = kspec_ref[block - source, imag_rows, :]
            v_re = vspec_ref[source, real_rows, :]
            v_im = vspec_ref[source, imag_rows, :]
            real = real + (k_re * v_re - k_im * v_im)
            imag = imag + (k_re * v_im + k_im * v_re)
        acc_ref[real_rows, :] = real
        acc_ref[imag_rows, :] = imag
        return carry

    lax.fori_loop(0, block_len // rows, chunk, 0)
    upper, lower = halves(acc_ref[...])
    return mm(back_table, jnp.concatenate([upper, lower, upper], axis=0))


PIECE = 256


def layer_body(
    seq_count, chips,
    tokens_ref, w_up_ref, w_out_ref, rpe_out_ref, small_ref, enc_ref, map_ref, tables_ref,
    out_ref,
    up_w, out_w, rpe_v, small_v, enc_v, map_v, tables_v,
    seq_x, chan_x, kspec_ref, vspec_ref, acc_ref, toep_out, toep_in, gate_ref, hidden_ref,
    give_out, give_in, cross_out, cross_in, own_sum,
    load_sems, xs_send, xs_recv, ag_send, ag_recv, fw_send, fw_recv, tb_send, tb_recv,
    gv_send, gv_recv, cr_send, cr_recv,
):
    mesh_ids = pl.DeviceIdType.MESH
    me = lax.axis_index("seq")
    chan = lax.axis_index("chan")
    chip, core = chan // 2, chan % 2
    partner = chip * 2 + (1 - core)
    block_len, chans = tokens_ref.shape[2], tokens_ref.shape[3]
    width = chans // seq_count
    total = 2 * seq_count
    own_tokens = tokens_ref.at[0]

    def remote(source, target, send, recv, device):
        return pltpu.make_async_remote_copy(
            src_ref=source, dst_ref=target, send_sem=send, recv_sem=recv,
            device_id=device, device_id_type=mesh_ids,
        )

    def seq_ahead(offset):
        return lax.rem(me + offset, seq_count)

    def chip_ahead(offset):
        return lax.rem(chip + offset, chips)

    loads = [
        pltpu.make_async_copy(source, target, load_sems.at[i])
        for i, (source, target) in enumerate([
            (rpe_out_ref, rpe_v), (small_ref, small_v), (enc_ref, enc_v), (map_ref, map_v),
            (tables_ref, tables_v), (w_up_ref, up_w), (w_out_ref, out_w),
            (own_tokens, chan_x.at[chan]),
            (own_tokens.at[:, :, pl.ds(pl.multiple_of(me * width, width), width)], seq_x.at[me]),
        ])
    ]
    for load in loads[:5]:
        load.start()

    barrier = pltpu.get_barrier_semaphore()
    for offset in range(1, seq_count):
        pl.semaphore_signal(barrier, inc=1, device_id={"seq": seq_ahead(offset)}, device_id_type=mesh_ids)
    pl.semaphore_signal(barrier, inc=1, device_id={"chan": partner}, device_id_type=mesh_ids)
    for offset in range(1, chips):
        pl.semaphore_signal(
            barrier, inc=1, device_id={"chan": chip_ahead(offset) * 2 + core}, device_id_type=mesh_ids
        )
    pl.semaphore_wait(barrier, seq_count - 1 + 1 + chips - 1)

    exchange = []
    for offset in range(1, seq_count):
        target = seq_ahead(offset)
        exchange.append(remote(
            own_tokens.at[:, :, pl.ds(pl.multiple_of(target * width, width), width)], seq_x.at[me],
            xs_send.at[offset - 1], xs_recv.at[offset - 1], {"seq": target},
        ))
    gather = []
    for offset in range(1, chips):
        gather.append(remote(
            own_tokens, chan_x.at[chan], ag_send.at[offset], ag_recv.at[offset],
            {"chan": chip_ahead(offset) * 2 + core},
        ))
    gather.append(remote(own_tokens, chan_x.at[chan], ag_send.at[0], ag_recv.at[0], {"chan": partner}))
    for copy in exchange + gather:
        copy.start()
    for load in loads[5:]:
        load.start()

    for load in loads[:5]:
        load.wait()
    hidden_dim = rpe_v.shape[0]
    rim = 4
    start = pl.multiple_of(chan * chans + me * width, width)
    table = jnp.concatenate([rpe_v[...], small_v[...]], axis=0)
    selected, counts = select_params(table, map_v[:, pl.ds(start, width)], map_v[...], hidden_dim)
    double_len = 2 * block_len
    toep_kernel_spectra(
        selected, enc_v[hidden_dim : hidden_dim + 1], enc_v[hidden_dim + 1 : hidden_dim + 2],
        enc_v[:hidden_dim], tables_v[:double_len, : 3 * double_len], kspec_ref,
        total * block_len, block_len,
    )
    taps = selected[hidden_dim + 1 : hidden_dim + 2 + rim]
    scale = 1.0 / counts

    loads[8].wait()
    for copy in exchange:
        copy.wait()
    convolve_blocks(seq_x, taps, tables_v[:double_len, 3 * double_len :], vspec_ref)

    forwards = []
    for offset in range(1, chips):
        gather[offset - 1].wait()
        origin = lax.rem(chip + chips - offset, chips) * 2 + core
        forward = remote(
            chan_x.at[origin], chan_x.at[origin], fw_send.at[offset], fw_recv.at[offset], {"chan": partner}
        )
        forward.start()
        forwards.append(forward)

    back_table = tables_v[double_len:, : 3 * double_len]
    for block in range(total):
        toep = (mix_block(block, kspec_ref, vspec_ref, acc_ref, back_table) * scale).astype(BF)
        dest, half = place_of(block, seq_count)
        toep_out[dest, half] = toep

        @pl.when(me != dest)
        def _():
            remote(
                toep_out.at[dest, half], toep_in.at[me, half], tb_send.at[dest, half],
                tb_recv.at[me, half], {"seq": dest},
            ).start()

        @pl.when(me == dest)
        def _():
            toep_in[me, half] = toep

    gather[-1].wait()
    for forward in forwards:
        forward.wait()
    for load in loads[5:8]:
        load.wait()

    tile = PIECE
    token_count = 2 * block_len

    def gate_tile(step, carry):
        columns = pl.ds(pl.multiple_of(step * tile, tile), tile)
        up = jnp.zeros((token_count, tile), F32)
        for origin in range(2 * chips):
            up = up + mm(
                chan_x[origin].reshape(token_count, chans), up_w[pl.ds(origin * chans, chans), columns]
            )
        gate_ref[:, columns] = up * jax.nn.sigmoid(up)
        return carry

    lax.fori_loop(0, chans // tile, gate_tile, 0)

    for source in range(seq_count):

        @pl.when(me != source)
        def _():
            for half in range(2):
                remote(
                    toep_out.at[source, half], toep_in.at[source, half], tb_send.at[source, half],
                    tb_recv.at[source, half], {"seq": source},
                ).wait()

        columns = slice(source * width, (source + 1) * width)
        hidden_ref[:, columns] = (
            gate_ref[:, columns] * toep_in[source].reshape(token_count, width).astype(F32)
        ).astype(BF)

    pieces = chans // tile

    def part(device, piece):
        columns = pl.ds(pl.multiple_of(device * chans + piece * tile, tile), tile)
        return mm(hidden_ref[...], out_w[:, columns])

    def give(slot, piece):
        return remote(
            give_out.at[slot, piece], give_in.at[slot, piece], gv_send.at[slot, piece],
            gv_recv.at[slot, piece], {"chan": partner},
        )

    def cross(slot, piece, offset):
        return remote(
            cross_out.at[slot, piece], cross_in.at[slot, piece], cr_send.at[slot, piece],
            cr_recv.at[slot, piece], {"chan": chip_ahead(offset) * 2 + core},
        )

    def each_piece(work):
        def step(piece, carry):
            work(piece)
            return carry

        lax.fori_loop(0, pieces, step, 0)

    def hand_over(offset):
        def work(piece):
            give_out[offset, piece] = part(chip_ahead(offset) * 2 + (1 - core), piece).astype(BF)
            give(offset, piece).start()

        each_piece(work)

    for offset in range(1, chips):
        hand_over(offset)

        def send_across(piece):
            mine = part(chip_ahead(offset) * 2 + core, piece)
            give(offset, piece).wait()
            cross_out[offset - 1, piece] = (mine + give_in[offset, piece].astype(F32)).astype(BF)
            cross(offset - 1, piece, offset).start()

        each_piece(send_across)
    hand_over(0)

    def keep(piece):
        own_sum[piece] = part(chan, piece)

    each_piece(keep)

    def finish(piece):
        give(0, piece).wait()
        result = own_sum[piece] + give_in[0, piece].astype(F32)
        for offset in range(1, chips):
            cross(offset - 1, piece, offset).wait()
            result = result + cross_in[offset - 1, piece].astype(F32)
        columns = pl.ds(pl.multiple_of(piece * tile, tile), tile)
        out_ref[0, :, :, columns] = result.astype(out_ref.dtype).reshape(2, block_len, tile)

    each_piece(finish)


def shards(
    tokens, w_up, w_out, rpe_in_w, rpe_in_b, rpe_mid_w, rpe_out_w, decay_rate, conv_taps, chan_map
):
    _, _, block_len, chans = tokens.shape
    seq_count = lax.axis_size("seq")
    chan_count = lax.axis_size("chan")
    chips = chan_count // 2
    total = 2 * seq_count
    width = chans // seq_count
    double_len = 2 * block_len
    pieces = chans // PIECE
    hidden_dim, old_count = rpe_out_w.shape
    small = jnp.concatenate([decay_rate[None, :], conv_taps], axis=0)
    small = jnp.pad(small, ((0, -small.shape[0] % 16), (0, 0)))
    encoder = jnp.concatenate([rpe_mid_w, rpe_in_w[None, :], rpe_in_b[None, :]], axis=0)
    encoder = jnp.pad(encoder, ((0, -encoder.shape[0] % 8), (0, 0)))
    kern_table, data_table, back_table = odd_tables(block_len)
    tables = np.concatenate(
        [
            np.concatenate([kern_table, data_table], axis=1),
            np.pad(back_table, ((0, 0), (0, double_len))),
        ],
        axis=0,
    )
    token_count = 2 * block_len
    vmem = pltpu.VMEM
    dma = pltpu.SemaphoreType.DMA
    return pl.pallas_call(
        functools.partial(layer_body, seq_count, chips),
        out_shape=jax.ShapeDtypeStruct(tokens.shape, BF),
        in_specs=[pl.BlockSpec(memory_space=pl.ANY)] * 8,
        out_specs=pl.BlockSpec(memory_space=pltpu.VMEM),
        scratch_shapes=[
            vmem(w_up.shape, BF),
            vmem(w_out.shape, BF),
            vmem(rpe_out_w.shape, F32),
            vmem(small.shape, F32),
            vmem(encoder.shape, F32),
            vmem((1, chan_map.shape[0]), jnp.int32),
            vmem(tables.shape, BF),
            vmem((seq_count, 2, block_len, width), BF),
            vmem((chan_count, 2, block_len, chans), BF),
            vmem((total, double_len, width), F32),
            vmem((total, double_len, width), F32),
            vmem((double_len, width), F32),
            vmem((seq_count, 2, block_len, width), BF),
            vmem((seq_count, 2, block_len, width), BF),
            vmem((token_count, chans), F32),
            vmem((token_count, chans), BF),
            vmem((chips, pieces, token_count, PIECE), BF),
            vmem((chips, pieces, token_count, PIECE), BF),
            vmem((chips - 1, pieces, token_count, PIECE), BF),
            vmem((chips - 1, pieces, token_count, PIECE), BF),
            vmem((pieces, token_count, PIECE), F32),
            dma((9,)),
            dma((seq_count - 1,)),
            dma((seq_count - 1,)),
            dma((chips,)),
            dma((chips,)),
            dma((chips,)),
            dma((chips,)),
            dma((seq_count, 2)),
            dma((seq_count, 2)),
            dma((chips, pieces)),
            dma((chips, pieces)),
            dma((chips - 1, pieces)),
            dma((chips - 1, pieces)),
        ],
        compiler_params=pltpu.CompilerParams(
            collective_id=0, has_side_effects=True, vmem_limit_bytes=58 * 1024 * 1024
        ),
    )(tokens, w_up, w_out, rpe_out_w, small, encoder, chan_map[None, :], tables)


def solution(mesh):
    in_specs = (
        P(("groups", "seq"), None, None, "chan"),
        P(None, "chan"),
        P("chan", None),
        P(),
        P(),
        P(),
        P(),
        P(),
        P(),
        P(),
    )
    out_specs = P(("groups", "seq"), None, None, "chan")
    def pick(*arrays):
        chans = arrays[0].shape[3]
        narrow = (chans // mesh.shape["seq"]) % 128 or chans % PIECE or mesh.shape["chan"] < 4
        return (general_shards if narrow else shards)(*arrays)

    return jax.shard_map(pick, mesh=mesh, in_specs=in_specs, out_specs=out_specs, check_vma=False)
```

```python
import functools
import math

import jax
import jax.numpy as jnp
import numpy as np
from jax import lax
from jax.experimental import pallas as pl
from jax.experimental.pallas import tpu as pltpu
from jax.sharding import PartitionSpec as P

HIGH = lax.Precision.HIGHEST


def shifted(x, axis, by):
    length = lax.axis_size(axis)
    pairs = [(i, i + by) for i in range(length) if 0 <= i + by < length]
    return lax.ppermute(x, axis, pairs)


def dft_tables(block_len):
    period_len = 2 * block_len
    freq_index = jnp.arange(block_len + 1, dtype=jnp.int32)[:, None]
    time_index = jnp.arange(block_len, dtype=jnp.int32)[None, :]
    angles = (freq_index * time_index % period_len).astype(jnp.float32) * (
        2.0 * math.pi / period_len
    )
    forward = jnp.concatenate([jnp.cos(angles), -jnp.sin(angles)], axis=0)
    weights = (
        jnp.where((freq_index == 0) | (freq_index == block_len), 1.0, 2.0).astype(jnp.float32)
        / period_len
    )
    inverse = jnp.concatenate(
        [(weights * jnp.cos(angles)).T, (-weights * jnp.sin(angles)).T], axis=1
    )
    sign_flip = jnp.where(freq_index[:, 0] % 2 == 0, 1.0, -1.0).astype(jnp.float32)
    return (forward, inverse, sign_flip)


def spectra_of(forward, blocks):
    freq_count = forward.shape[0] // 2
    spec = jnp.einsum("gb,hbc->hgc", forward, blocks, precision=HIGH)
    return spec.reshape(blocks.shape[0], 2, freq_count, blocks.shape[2])


def data_spectra(fwd_upper, fwd_lower, blocks):
    freq_count = fwd_upper.shape[0] // 2
    spec = jnp.einsum("gb,hbc->hgc", fwd_upper, blocks, preferred_element_type=jnp.float32)
    spec = spec + jnp.einsum("gb,hbc->hgc", fwd_lower, blocks, preferred_element_type=jnp.float32)
    return spec.reshape(blocks.shape[0], 2, freq_count, blocks.shape[2])


def accumulate(acc, spec_pair, source, own_ids, kernel_spec, total_blocks):
    src_ids = jnp.stack([source, total_blocks - 1 - source])
    lags = own_ids[:, None] - src_ids[None, :]
    valid = (lags >= 0).astype(jnp.float32)[:, :, None, None]
    picked = jnp.take(kernel_spec, jnp.clip(lags, 0, total_blocks - 1).reshape(-1), axis=0)
    picked = picked.reshape((2, 2) + kernel_spec.shape[1:])
    kern_real = picked[:, :, 0]
    kern_imag = picked[:, :, 1]
    data_real = spec_pair[None, :, 0]
    data_imag = spec_pair[None, :, 1]
    real_part = jnp.sum(valid * (kern_real * data_real - kern_imag * data_imag), axis=1)
    imag_part = jnp.sum(valid * (kern_real * data_imag + kern_imag * data_real), axis=1)
    return acc + jnp.stack([real_part, imag_part], axis=1)


def general_shards(
    tokens, w_up, w_out, rpe_in_w, rpe_in_b, rpe_mid_w, rpe_out_w, decay_rate, conv_taps, chan_map
):
    block_len = tokens.shape[2]
    chans = tokens.shape[3]
    seq_count = lax.axis_size("seq")
    seq_pos = lax.axis_index("seq")
    total_blocks = 2 * seq_count
    seq_len = total_blocks * block_len
    rim = conv_taps.shape[0] - 1
    old_count = decay_rate.shape[0]
    hidden_dim = rpe_out_w.shape[0]
    map_local = lax.dynamic_slice_in_dim(chan_map, lax.axis_index("chan") * chans, chans)
    counts = jnp.sum((map_local[:, None] == chan_map[None, :]).astype(jnp.float32), axis=1)
    one_hot = (jnp.arange(old_count, dtype=jnp.int32)[:, None] == map_local[None, :]).astype(
        jnp.float32
    )
    table = jnp.concatenate([rpe_out_w, decay_rate[None, :], conv_taps], axis=0)
    selected = jnp.dot(table, one_hot, precision=HIGH)
    out_cols = selected[:hidden_dim]
    rates = selected[hidden_dim]
    taps_local = selected[hidden_dim + 1 :]
    x_own = tokens[0]
    prev_low = shifted(tokens[:, 0, block_len - rim :], "seq", 1)[0]
    prev_high = shifted(tokens[:, 1, block_len - rim :], "seq", -1)[0]
    prev_high = jnp.where(seq_pos == seq_count - 1, x_own[0, block_len - rim :], prev_high)
    extended = jnp.stack(
        [
            jnp.concatenate([prev_low, x_own[0]], axis=0),
            jnp.concatenate([prev_high, x_own[1]], axis=0),
        ]
    ).astype(jnp.float32)
    conv = jnp.zeros((2, block_len, chans), jnp.float32)
    for shift_m in range(rim + 1):
        conv = (
            conv
            + taps_local[shift_m][None, None, :]
            * extended[:, rim - shift_m : rim - shift_m + block_len]
        )
    v_data = conv.astype(jnp.bfloat16)
    positions = jnp.arange(seq_len, dtype=jnp.int32).astype(jnp.float32)
    first = jax.nn.relu((positions / seq_len)[:, None] * rpe_in_w[None, :] + rpe_in_b[None, :])
    second = jax.nn.relu(jnp.dot(first, rpe_mid_w, precision=HIGH))
    encoded = jnp.dot(second, out_cols, precision=HIGH)
    gain = jnp.sqrt(2.0 * rates / (1.0 - jnp.exp(-2.0 * rates * seq_len)))
    kernel = encoded * jnp.exp(-rates[None, :] * positions[:, None]) * gain[None, :]
    forward, inverse, sign_flip = dft_tables(block_len)
    fwd_upper = forward.astype(jnp.bfloat16)
    fwd_lower = (forward - fwd_upper.astype(jnp.float32)).astype(jnp.bfloat16)
    half_spec = spectra_of(forward, kernel.reshape(total_blocks, block_len, chans))
    earlier = jnp.concatenate([jnp.zeros_like(half_spec[:1]), half_spec[:-1]], axis=0)
    kernel_spec = half_spec + sign_flip[None, None, :, None] * earlier
    own_ids = jnp.stack([seq_pos, total_blocks - 1 - seq_pos])
    start_acc = jnp.zeros((2, 2, block_len + 1, chans), jnp.float32)
    piece = lax.all_gather(v_data[None], "seq", axis=0, tiled=True)

    def one_source(carry, item):
        offset, blocks = item
        spec_pair = data_spectra(fwd_upper, fwd_lower, blocks)
        return (accumulate(carry, spec_pair, offset, own_ids, kernel_spec, total_blocks), None)

    offsets = jnp.arange(piece.shape[0], dtype=jnp.int32)
    result, _ = lax.scan(one_source, start_acc, (offsets, piece))
    toep = jnp.einsum(
        "tg,agc->atc", inverse, result.reshape(2, 2 * (block_len + 1), chans), precision=HIGH
    )
    up_pre = jnp.einsum(
        "qhbc,cd->qhbd",
        lax.all_gather(tokens, "chan", axis=3, tiled=True),
        w_up,
        preferred_element_type=jnp.float32,
    )
    hidden = (jax.nn.silu(up_pre) * toep[None] / counts[None, None, None, :]).astype(jnp.bfloat16)
    partial_sum = jnp.einsum("qhbc,cd->qhbd", hidden, w_out, preferred_element_type=jnp.float32)
    return lax.psum_scatter(partial_sum, "chan", scatter_dimension=3, tiled=True).astype(
        jnp.bfloat16
    )


BF = jnp.bfloat16
F32 = jnp.float32
LOW = 64


def halves(x):
    upper = x.astype(BF)
    return upper, (x - upper.astype(F32)).astype(BF)


def odd_tables(block_len):
    omega = 2.0 * np.pi * (np.arange(block_len)[:, None] + 0.5) / (2 * block_len)
    lags = np.arange(-block_len, block_len)[None, :]
    kern_table = np.concatenate([np.cos(omega * lags), -np.sin(omega * lags)], axis=0)
    data_table = kern_table[:, block_len:]
    times = np.arange(block_len)[None, :]
    back_table = np.concatenate([np.cos(omega * times), -np.sin(omega * times)], axis=0).T / block_len

    def split(table):
        table = table.astype(np.float32)
        upper = table.astype(BF)
        return upper, (table - upper.astype(np.float32)).astype(BF)

    kern_upper, kern_lower = split(kern_table)
    data_upper, data_lower = split(data_table)
    back_upper, back_lower = split(back_table)
    return (
        np.concatenate([kern_upper, kern_upper, kern_lower], axis=1),
        np.concatenate([data_upper, data_lower], axis=1),
        np.concatenate([back_upper, back_upper, back_lower], axis=1),
    )


def mm(a, b):
    return jnp.dot(a, b, preferred_element_type=F32)


def select_params(table, old_of_own, chan_map_row, hidden_dim):
    rows, old_count = table.shape
    width = old_of_own.shape[1]
    upper = table.astype(BF)
    rest = table - upper.astype(F32)
    middle = rest.astype(BF)
    lower = (rest - middle.astype(F32)).astype(BF)
    one_hot = jnp.where(
        lax.broadcasted_iota(jnp.int32, (old_count, width), 0) == old_of_own, 1.0, 0.0
    ).astype(BF)
    selected = mm(upper, one_hot) + mm(middle, one_hot) + mm(lower, one_hot)
    high_count = -(-old_count // LOW)

    def digits(ids):
        width = ids.shape[1]
        high_hot = jnp.where(
            lax.broadcasted_iota(jnp.int32, (high_count, width), 0) == (ids >> 6), 1.0, 0.0
        )
        low_hot = jnp.where(
            lax.broadcasted_iota(jnp.int32, (LOW, width), 0) == (ids & (LOW - 1)), 1.0, 0.0
        )
        return high_hot, low_hot.astype(BF)

    all_high, all_low = digits(chan_map_row)
    histogram = lax.dot_general(
        all_high.astype(BF), all_low, (((1,), (1,)), ((), ())), preferred_element_type=F32
    )
    own_high, own_low = digits(old_of_own)
    hist_upper, hist_lower = halves(histogram)
    counts = jnp.sum(own_high * (mm(hist_upper, own_low) + mm(hist_lower, own_low)), axis=0, keepdims=True)
    return selected, counts


def toep_kernel_spectra(selected, in_w, in_b, mid_w, kern_table, kspec_ref, seq_len, block_len):
    hidden_dim = mid_w.shape[0]
    width = selected.shape[1]
    rates = selected[hidden_dim : hidden_dim + 1]
    positions = lax.broadcasted_iota(jnp.int32, (seq_len, 1), 0).astype(F32)
    first = jnp.maximum((positions / seq_len) * in_w + in_b, 0.0)
    second = jnp.maximum(jnp.dot(first, mid_w, precision=HIGH, preferred_element_type=F32), 0.0)
    encoded = jnp.dot(second, selected[:hidden_dim], precision=HIGH, preferred_element_type=F32)
    gain = jnp.sqrt(2.0 * rates / (1.0 - jnp.exp(-2.0 * rates * seq_len)))
    kern = encoded * jnp.exp(-rates * positions) * gain
    upper, lower = halves(kern)
    blank = jnp.zeros((block_len, width), BF)
    upper = jnp.concatenate([blank, upper], axis=0)
    lower = jnp.concatenate([blank, lower], axis=0)
    for lag in range(seq_len // block_len):
        span = slice(lag * block_len, (lag + 2) * block_len)
        stacked = jnp.concatenate([upper[span], lower[span], upper[span]], axis=0)
        kspec_ref[lag] = mm(kern_table, stacked)


def convolve_block(block, x_ref, taps, data_table, vspec_ref):
    seq_count, _, block_len, width = x_ref.shape
    rim = taps.shape[0] - 1
    own = x_ref[place_of(block, seq_count)].astype(F32)
    if block:
        source, half = place_of(block - 1, seq_count)
        tail = x_ref[source, half, block_len - 16 :, :].astype(F32)[8:]
    else:
        tail = jnp.zeros((8, width), F32)
    extended = jnp.concatenate([tail, own], axis=0)
    conv = taps[0:1] * own
    for shift in range(1, rim + 1):
        conv = conv + taps[shift : shift + 1] * extended[8 - shift : 8 - shift + block_len]
    v_data = conv.astype(BF)
    vspec_ref[block] = mm(data_table, jnp.concatenate([v_data, v_data], axis=0))


def place_of(block, seq_count):
    return (block, 0) if block < seq_count else (2 * seq_count - 1 - block, 1)


def mix_block(block, kspec_ref, vspec_ref, acc_ref, back_table):
    total, double_len, width = vspec_ref.shape
    block_len = double_len // 2
    rows = 32

    def chunk(step, carry):
        start = pl.multiple_of(step * rows, rows)
        real_rows = pl.ds(start, rows)
        imag_rows = pl.ds(pl.multiple_of(start + block_len, rows), rows)
        real = jnp.zeros((rows, width), F32)
        imag = jnp.zeros((rows, width), F32)
        for source in range(block + 1):
            k_re = kspec_ref[block - source, real_rows, :]
            k_im = kspec_ref[block - source, imag_rows, :]
            v_re = vspec_ref[source, real_rows, :]
            v_im = vspec_ref[source, imag_rows, :]
            real = real + (k_re * v_re - k_im * v_im)
            imag = imag + (k_re * v_im + k_im * v_re)
        acc_ref[real_rows, :] = real
        acc_ref[imag_rows, :] = imag
        return carry

    lax.fori_loop(0, block_len // rows, chunk, 0)
    upper, lower = halves(acc_ref[...])
    return mm(back_table, jnp.concatenate([upper, lower, upper], axis=0))


PIECE = 256


def layer_body(
    seq_count, chips,
    tokens_ref, w_up_ref, w_out_ref, rpe_out_ref, rate_ref, taps_ref, in_w_ref, in_b_ref, mid_ref,
    map_ref, tables_ref,
    out_ref,
    up_w, out_w, rpe_v, rate_v, taps_v, in_w_v, in_b_v, mid_v, map_v, tables_v,
    seq_x, chan_x, kspec_ref, vspec_ref, acc_ref, toep_out, toep_in, gate_ref, hidden_ref,
    give_out, give_in, cross_out, cross_in, own_sum,
    load_sems, xs_send, xs_recv, ag_send, ag_recv, fw_send, fw_recv, tb_send, tb_recv,
    gv_send, gv_recv, cr_send, cr_recv,
):
    mesh_ids = pl.DeviceIdType.MESH
    me = lax.axis_index("seq")
    chan = lax.axis_index("chan")
    chip, core = chan // 2, chan % 2
    partner = chip * 2 + (1 - core)
    block_len, chans = tokens_ref.shape[2], tokens_ref.shape[3]
    width = chans // seq_count
    total = 2 * seq_count
    own_tokens = tokens_ref.at[0]

    def remote(source, target, send, recv, device):
        return pltpu.make_async_remote_copy(
            src_ref=source, dst_ref=target, send_sem=send, recv_sem=recv,
            device_id=device, device_id_type=mesh_ids,
        )

    def seq_ahead(offset):
        return lax.rem(me + offset, seq_count)

    def chip_ahead(offset):
        return lax.rem(chip + offset, chips)

    loads = [
        pltpu.make_async_copy(source, target, load_sems.at[i])
        for i, (source, target) in enumerate([
            (rpe_out_ref, rpe_v), (rate_ref, rate_v), (taps_ref, taps_v), (in_w_ref, in_w_v),
            (in_b_ref, in_b_v), (mid_ref, mid_v), (map_ref, map_v), (tables_ref, tables_v), (w_up_ref, up_w), (w_out_ref, out_w),
            (own_tokens, chan_x.at[chan]),
            (own_tokens.at[:, :, pl.ds(pl.multiple_of(me * width, width), width)], seq_x.at[me]),
        ])
    ]
    for load in loads[:8]:
        load.start()

    barrier = pltpu.get_barrier_semaphore()
    for offset in range(1, seq_count):
        pl.semaphore_signal(barrier, inc=1, device_id={"seq": seq_ahead(offset)}, device_id_type=mesh_ids)
    pl.semaphore_signal(barrier, inc=1, device_id={"chan": partner}, device_id_type=mesh_ids)
    for offset in range(1, chips):
        pl.semaphore_signal(
            barrier, inc=1, device_id={"chan": chip_ahead(offset) * 2 + core}, device_id_type=mesh_ids
        )
    pl.semaphore_wait(barrier, seq_count - 1 + 1 + chips - 1)

    exchange, gather = ([], []), ([], [])
    for half in range(2):
        for offset in range(1, seq_count):
            target = seq_ahead(offset)
            columns = pl.ds(pl.multiple_of(target * width, width), width)
            exchange[half].append(remote(
                own_tokens.at[half, :, columns], seq_x.at[me, half],
                xs_send.at[offset - 1, half], xs_recv.at[offset - 1, half], {"seq": target},
            ))
        for offset in range(1, chips):
            gather[half].append(remote(
                own_tokens.at[half], chan_x.at[chan, half], ag_send.at[offset, half],
                ag_recv.at[offset, half], {"chan": chip_ahead(offset) * 2 + core},
            ))
        gather[half].append(remote(
            own_tokens.at[half], chan_x.at[chan, half], ag_send.at[0, half], ag_recv.at[0, half],
            {"chan": partner},
        ))
        for copy in exchange[half] + gather[half]:
            copy.start()
    for load in loads[8:]:
        load.start()

    for load in loads[:8]:
        load.wait()
    hidden_dim = rpe_v.shape[0]
    rim = taps_v.shape[0] - 1
    start = pl.multiple_of(chan * chans + me * width, width)
    small = jnp.concatenate(
        [rate_v[...], taps_v[...], jnp.zeros((16 - 2 - rim, rate_v.shape[1]), F32)], axis=0
    )
    table = jnp.concatenate([rpe_v[...], small], axis=0)
    selected, counts = select_params(table, map_v[:, pl.ds(start, width)], map_v[...], hidden_dim)
    double_len = 2 * block_len
    toep_kernel_spectra(
        selected, in_w_v[...], in_b_v[...], mid_v[...], tables_v[:double_len, : 3 * double_len], kspec_ref,
        total * block_len, block_len,
    )
    taps = selected[hidden_dim + 1 : hidden_dim + 2 + rim]
    scale = 1.0 / counts

    data_table = tables_v[:double_len, 3 * double_len :]
    back_table = tables_v[double_len:, : 3 * double_len]
    tile = PIECE
    pieces = chans // tile

    def back(dest, half):
        return remote(
            toep_out.at[dest, half], toep_in.at[me, half], tb_send.at[dest, half],
            tb_recv.at[me, half], {"seq": dest},
        )

    def receive(half):
        for copy in exchange[half]:
            copy.wait()
        for block in range(half * seq_count, (half + 1) * seq_count):
            convolve_block(block, seq_x, taps, data_table, vspec_ref)

    def mix(block):
        toep = (mix_block(block, kspec_ref, vspec_ref, acc_ref, back_table) * scale).astype(BF)
        dest, half = place_of(block, seq_count)
        toep_out[dest, half] = toep

        @pl.when(me != dest)
        def _():
            back(dest, half).start()

        @pl.when(me == dest)
        def _():
            toep_in[me, half] = toep

    def forward(offset, half):
        origin = lax.rem(chip + chips - offset, chips) * 2 + core
        return remote(
            chan_x.at[origin, half], chan_x.at[origin, half], fw_send.at[offset, half],
            fw_recv.at[offset, half], {"chan": partner},
        )

    def pass_on(half):
        for offset in range(1, chips):
            gather[half][offset - 1].wait()
            forward(offset, half).start()

    def gate(half):
        gather[half][-1].wait()
        for offset in range(1, chips):
            forward(offset, half).wait()

        def gate_tile(step, carry):
            columns = pl.ds(pl.multiple_of(step * tile, tile), tile)
            up = jnp.zeros((block_len, tile), F32)
            for origin in range(2 * chips):
                up = up + mm(chan_x[origin, half], up_w[pl.ds(origin * chans, chans), columns])
            gate_ref[half, :, columns] = up * jax.nn.sigmoid(up)
            return carry

        lax.fori_loop(0, pieces, gate_tile, 0)

    def combine(half):
        for source in range(seq_count):

            @pl.when(me != source)
            def _():
                remote(
                    toep_out.at[source, half], toep_in.at[source, half], tb_send.at[source, half],
                    tb_recv.at[source, half], {"seq": source},
                ).wait()

            columns = slice(source * width, (source + 1) * width)
            hidden_ref[half, :, columns] = (
                gate_ref[half, :, columns] * toep_in[source, half].astype(F32)
            ).astype(BF)

    def part(device, half, piece):
        columns = pl.ds(pl.multiple_of(device * chans + piece * tile, tile), tile)
        return mm(hidden_ref[half], out_w[:, columns])

    def give(slot, half, piece):
        return remote(
            give_out.at[half, slot, piece], give_in.at[half, slot, piece],
            gv_send.at[half, slot, piece], gv_recv.at[half, slot, piece], {"chan": partner},
        )

    def cross(offset, half, piece):
        return remote(
            cross_out.at[half, offset - 1, piece], cross_in.at[half, offset - 1, piece],
            cr_send.at[half, offset - 1, piece], cr_recv.at[half, offset - 1, piece],
            {"chan": chip_ahead(offset) * 2 + core},
        )

    def each_piece(work):
        def step(piece, carry):
            work(piece)
            return carry

        lax.fori_loop(0, pieces, step, 0)

    def hand_over(offset, half):
        def work(piece):
            device = chip_ahead(offset) * 2 + (1 - core)
            give_out[half, offset, piece] = part(device, half, piece).astype(BF)
            give(offset, half, piece).start()

        each_piece(work)

    def project(half):
        for offset in range(1, chips):
            hand_over(offset, half)

            def send_across(piece):
                mine = part(chip_ahead(offset) * 2 + core, half, piece)
                give(offset, half, piece).wait()
                total_of_chip = mine + give_in[half, offset, piece].astype(F32)
                cross_out[half, offset - 1, piece] = total_of_chip.astype(BF)
                cross(offset, half, piece).start()

            each_piece(send_across)
        hand_over(0, half)

        def keep(piece):
            own_sum[half, piece] = part(chan, half, piece)

        each_piece(keep)

    def finish(half):
        def work(piece):
            give(0, half, piece).wait()
            result = own_sum[half, piece] + give_in[half, 0, piece].astype(F32)
            for offset in range(1, chips):
                cross(offset, half, piece).wait()
                result = result + cross_in[half, offset - 1, piece].astype(F32)
            columns = pl.ds(pl.multiple_of(piece * tile, tile), tile)
            out_ref[0, half, :, columns] = result.astype(out_ref.dtype)

        each_piece(work)

    loads[11].wait()
    receive(0)
    for block in range(seq_count):
        mix(block)
    pass_on(0)
    loads[8].wait()
    loads[10].wait()
    gate(0)
    receive(1)
    for block in range(seq_count, total):
        mix(block)
        if block == total - 2:
            pass_on(1)
    loads[9].wait()
    combine(0)
    project(0)
    gate(1)
    combine(1)
    project(1)
    finish(0)
    finish(1)


def shards(
    tokens, w_up, w_out, rpe_in_w, rpe_in_b, rpe_mid_w, rpe_out_w, decay_rate, conv_taps, chan_map
):
    _, _, block_len, chans = tokens.shape
    seq_count = lax.axis_size("seq")
    chan_count = lax.axis_size("chan")
    chips = chan_count // 2
    total = 2 * seq_count
    width = chans // seq_count
    double_len = 2 * block_len
    pieces = chans // PIECE
    hidden_dim, old_count = rpe_out_w.shape
    kern_table, data_table, back_table = odd_tables(block_len)
    tables = np.concatenate(
        [
            np.concatenate([kern_table, data_table], axis=1),
            np.pad(back_table, ((0, 0), (0, double_len))),
        ],
        axis=0,
    )
    vmem = pltpu.VMEM
    dma = pltpu.SemaphoreType.DMA
    return pl.pallas_call(
        functools.partial(layer_body, seq_count, chips),
        out_shape=jax.ShapeDtypeStruct(tokens.shape, BF),
        in_specs=[pl.BlockSpec(memory_space=pl.ANY)] * 11,
        out_specs=pl.BlockSpec(memory_space=pltpu.VMEM),
        scratch_shapes=[
            vmem(w_up.shape, BF),
            vmem(w_out.shape, BF),
            vmem(rpe_out_w.shape, F32),
            vmem((1, old_count), F32),
            vmem(conv_taps.shape, F32),
            vmem((1, hidden_dim), F32),
            vmem((1, hidden_dim), F32),
            vmem(rpe_mid_w.shape, F32),
            vmem((1, chan_map.shape[0]), jnp.int32),
            vmem(tables.shape, BF),
            vmem((seq_count, 2, block_len, width), BF),
            vmem((chan_count, 2, block_len, chans), BF),
            vmem((total, double_len, width), F32),
            vmem((total, double_len, width), F32),
            vmem((double_len, width), F32),
            vmem((seq_count, 2, block_len, width), BF),
            vmem((seq_count, 2, block_len, width), BF),
            vmem((2, block_len, chans), F32),
            vmem((2, block_len, chans), BF),
            vmem((2, chips, pieces, block_len, PIECE), BF),
            vmem((2, chips, pieces, block_len, PIECE), BF),
            vmem((2, chips - 1, pieces, block_len, PIECE), BF),
            vmem((2, chips - 1, pieces, block_len, PIECE), BF),
            vmem((2, pieces, block_len, PIECE), F32),
            dma((12,)),
            dma((seq_count - 1, 2)),
            dma((seq_count - 1, 2)),
            dma((chips, 2)),
            dma((chips, 2)),
            dma((chips, 2)),
            dma((chips, 2)),
            dma((seq_count, 2)),
            dma((seq_count, 2)),
            dma((2, chips, pieces)),
            dma((2, chips, pieces)),
            dma((2, chips - 1, pieces)),
            dma((2, chips - 1, pieces)),
        ],
        compiler_params=pltpu.CompilerParams(
            collective_id=0, has_side_effects=True, vmem_limit_bytes=58 * 1024 * 1024
        ),
    )(
        tokens, w_up, w_out, rpe_out_w, decay_rate[None, :], conv_taps, rpe_in_w[None, :],
        rpe_in_b[None, :], rpe_mid_w, chan_map[None, :], tables,
    )


def solution(mesh):
    in_specs = (
        P(("groups", "seq"), None, None, "chan"),
        P(None, "chan"),
        P("chan", None),
        P(),
        P(),
        P(),
        P(),
        P(),
        P(),
        P(),
    )
    out_specs = P(("groups", "seq"), None, None, "chan")
    def pick(*arrays):
        chans = arrays[0].shape[3]
        narrow = (chans // mesh.shape["seq"]) % 128 or chans % PIECE or mesh.shape["chan"] < 4
        return (general_shards if narrow else shards)(*arrays)

    return jax.shard_map(pick, mesh=mesh, in_specs=in_specs, out_specs=out_specs, check_vma=False)
```
